32 devices in a mesh: parts: 2 (over x), ulysses: 16 (over z, y, core).
Axes of the slice: x: 2, y: 2, z: 4, core: 2. Of those that a mesh axis runs over, the one named last changes fastest.
Arguments:
- query: bfloat16 [4096, 5120], P(('parts', 'ulysses')), parts along dimension 0, may hold values from -64 to 64
- key: bfloat16 [4096, 5120], P(('parts', 'ulysses')), parts along dimension 0, may hold values from -64 to 64
- value: bfloat16 [4096, 5120], P(('parts', 'ulysses')), parts along dimension 0, may hold values from -6 to 6
- query_gain: float32 [5120], replicated, may hold values from 1 to 4
- key_gain: float32 [5120], replicated, may hold values from 1 to 4
- key_blocks: int32 [80, 16, 12], P('parts'), parts along dimension 0, may hold values from 0 to 15, as said below
- block_counts: int32 [80, 16], P('parts'), parts along dimension 0, may hold values from 1 to 12, as said below
Outputs:
- attended: bfloat16 [4096, 5120], P(('parts', 'ulysses')), parts along dimension 0
The draws below stay inside these ranges and needn't reach their ends.
There are 2 independent parts, one for each index of `parts`. The reference program is written for one: setup_inputs(seed, part) draws one part's arguments, and reference() takes and returns one part's arrays. A program takes and returns all parts, laid end to end along the dimension named above; an argument that names none is the same for every part. Nothing has to cross between parts.
Inputs may be any that keep to these rules, and one draw needn't show every extreme that they name: `key_blocks`: each row of 12 entries lists different key blocks, the first one being the query block itself. `block_counts`: some row of every draw attends all 12 listed blocks.
All inputs are finite; a program needn't handle non-finite values.
Results may differ from the reference program's by a relative error of at most 0.0013.
The reference program's roundings to bfloat16 on the way count: a program that leaves them out, or rounds other values in their place, can miss the bound.
Values may be sent and summed in bfloat16 or wider, within the bound.
No kernel may reach another device: no remote copies, remote signals or barrier semaphores. Data moves between devices by JAX's collectives and lax.ppermute only.
A program may use at most 128 MiB of HBM per device.

```python
import math
import jax
import jax.numpy as jnp
from jax import lax

HEADS = 40
HEAD_DIM = 128
D = 5120
TILE = 128
KMAX = 12
TOKENS = 2048


def shared_parts(key):
    pieces = jax.random.split(key, 3)
    row_scale = jnp.exp(jax.random.uniform(pieces[0], (TOKENS, 1), jnp.float32, 0.0, math.log(10.0)))
    col_scale = 0.1 * jnp.exp(jax.random.uniform(pieces[1], (1, D), jnp.float32, 0.0, math.log(10.0)))
    normal_base = jax.random.normal(pieces[2], (TOKENS, D), jnp.float32)
    return (row_scale, col_scale, normal_base)


def draw_key(key, part):
    row_scale, col_scale, normal_base = shared_parts(key)
    field = normal_base * row_scale * col_scale
    return jnp.clip(field, -64.0, 64.0).astype(jnp.bfloat16)


def draw_query(key, part):
    row_scale, col_scale, normal_base = shared_parts(key)
    key = jax.random.fold_in(key, 9)
    pieces = jax.random.split(key, 2)
    own_rows = jnp.exp(jax.random.uniform(pieces[0], (TOKENS, 1), jnp.float32, 0.0, math.log(10.0)))
    field = jax.random.normal(pieces[1], (TOKENS, D), jnp.float32) * own_rows * col_scale
    return jnp.clip(field, -64.0, 64.0).astype(jnp.bfloat16)


def draw_key_blocks(key, part):
    key = jax.random.fold_in(key, 21)
    block_total = TOKENS // TILE
    noise = jax.random.randint(key, (HEADS, block_total, block_total), 0, 1 << 16)
    columns = jnp.arange(block_total, dtype=jnp.int32)
    order_key = noise * block_total + columns[None, None, :]
    own_block = columns[None, :, None] == columns[None, None, :]
    order_key = jnp.where(own_block, -1, order_key)
    return jnp.argsort(order_key, axis=-1, stable=True)[:, :, :KMAX].astype(jnp.int32)


def draw_block_counts(key, part):
    key = jax.random.fold_in(key, 22)
    pieces = jax.random.split(key, 3)
    block_total = TOKENS // TILE
    caps = jax.random.randint(pieces[0], (HEADS, 1), 1, KMAX + 1)
    raw = jax.random.randint(pieces[1], (HEADS, block_total), 0, 1 << 20)
    counts = 1 + raw % caps
    heavy = jax.random.randint(pieces[2], (), 0, HEADS)
    row_ids = jnp.arange(HEADS, dtype=jnp.int32)[:, None]
    col_ids = jnp.arange(block_total, dtype=jnp.int32)[None, :]
    counts = jnp.where((row_ids == heavy) & (col_ids == 0), KMAX, counts)
    return counts.astype(jnp.int32)


def level_of(stream_key, dims, cuts, least, largest):
    def one(dim, shards_of):
        steps = jax.random.uniform(jax.random.fold_in(jax.random.fold_in(stream_key, 6), dim), (shards_of,), jnp.float32, least / len(cuts), largest / len(cuts))
        return jnp.repeat(jnp.exp(steps), dims[dim] // shards_of).reshape((-1,) + (1,) * (len(dims) - dim - 1))

    level = one(*cuts[0])
    for cut in cuts[1:]:
        level = level * one(*cut)
    return level


def normal_values(own_key, extent, scale, bound, shards=(), held_as=jnp.bfloat16):
    loudness = level_of(own_key, extent, shards, -0.22, 0.18) if shards else 1.0
    values = jax.random.normal(own_key, extent, jnp.float32) * scale * loudness
    return jnp.minimum(jnp.maximum(values, -bound), bound).astype(held_as)


def setup_inputs(seed: int = 0, part: int = 0) -> dict:
    keys = jax.random.split(jax.random.key(seed), 8)
    part_keys = jax.random.split(jax.random.fold_in(keys[7], part), 8)
    query = draw_query(jax.random.fold_in(jax.random.fold_in(keys[7], part), 71), part)
    key = draw_key(jax.random.fold_in(jax.random.fold_in(keys[7], part), 71), part)
    value = normal_values(part_keys[2], (TOKENS, D), 1.0, 6.0, ((0, 16),))
    query_gain = jnp.clip(jnp.exp(jax.random.uniform(keys[3], (D,), jnp.float32, math.log(1.0), math.log(4.0))), 1.0, 4.0)
    key_gain = jnp.clip(jnp.exp(jax.random.uniform(keys[4], (D,), jnp.float32, math.log(1.0), math.log(4.0))), 1.0, 4.0)
    key_blocks = draw_key_blocks(jax.random.fold_in(jax.random.fold_in(keys[7], part), 71), part)
    block_counts = draw_block_counts(jax.random.fold_in(jax.random.fold_in(keys[7], part), 71), part)
    return {"query": query, "key": key, "value": value, "query_gain": query_gain, "key_gain": key_gain, "key_blocks": key_blocks, "block_counts": block_counts}


NORM_EPS = 1e-06

def rms_norm(values_in, gain):
    widened = values_in.astype(jnp.float32)
    inverse = lax.rsqrt(lax.optimization_barrier(jnp.mean(widened * widened, axis=-1, keepdims=True)) + NORM_EPS)
    return (widened * inverse * gain).astype(jnp.bfloat16)

def reference(query, key, value, query_gain, key_gain, key_blocks, block_counts):
    q_normed = lax.optimization_barrier(rms_norm(query, query_gain)).astype(jnp.float32)
    k_normed = lax.optimization_barrier(rms_norm(key, key_gain)).astype(jnp.float32)
    values_wide = value.astype(jnp.float32)
    block_total = TOKENS // TILE
    q_heads = q_normed.reshape(block_total, TILE, HEADS, HEAD_DIM)
    k_heads = k_normed.reshape(block_total, TILE, HEADS, HEAD_DIM)
    v_heads = values_wide.reshape(block_total, TILE, HEADS, HEAD_DIM)
    softmax_scale = HEAD_DIM ** (-0.5)

    def one_head(head):
        query_matrix = lax.dynamic_index_in_dim(q_heads, head, 2, keepdims=False)
        keys_all = lax.dynamic_index_in_dim(k_heads, head, 2, keepdims=False)
        values_all = lax.dynamic_index_in_dim(v_heads, head, 2, keepdims=False)
        key_lists = lax.dynamic_index_in_dim(key_blocks, head, 0, keepdims=False)
        live_count = lax.dynamic_index_in_dim(block_counts, head, 0, keepdims=False)
        key_panels = keys_all[key_lists]
        value_panels = values_all[key_lists]
        logit_matrix = jnp.einsum('frw,fgsw->frgs', query_matrix, key_panels) * softmax_scale
        live_mask = (jnp.arange(KMAX, dtype=jnp.int32)[None, :] < live_count[:, None])[:, None, :, None]
        logit_matrix = jnp.where(live_mask, logit_matrix, -1e+30)
        row_peak = lax.optimization_barrier(jnp.max(logit_matrix, axis=(2, 3), keepdims=True))
        weights = jnp.where(live_mask, jnp.exp(logit_matrix - row_peak), 0.0)
        row_denominator = lax.optimization_barrier(jnp.sum(weights, axis=(2, 3)))
        quantized_scores = lax.optimization_barrier(weights.astype(jnp.bfloat16)).astype(jnp.float32)
        blended_output = jnp.einsum('uenf,unfw->uew', quantized_scores, value_panels) / row_denominator[:, :, None]
        return blended_output.astype(jnp.bfloat16)
    per_head = lax.map(one_head, jnp.arange(HEADS, dtype=jnp.int32))
    return per_head.transpose(1, 2, 0, 3).reshape(TOKENS, HEADS * HEAD_DIM)
```

```python
import functools
import math

import jax
import jax.numpy as jnp
from jax import lax
from jax.experimental import pallas as pl
from jax.experimental.pallas import tpu as pltpu
from jax.sharding import PartitionSpec as P

HEADS = 40
HEAD_DIM = 128
TILE = 128
KMAX = 12
HALF = TILE // 2

NORM_EPS = 1e-06
MASKED = -1e30
EXP2_SCALE = HEAD_DIM ** (-0.5) * math.log2(math.e)
UNROLLS = (1, 2, 3, 4, 6, 8, 10, 12)
VMEM_LIMIT = 48 * 1024 * 1024

ROWS_X = 3 * TILE + HALF + TILE
ROWS_Y = 3 * TILE

ANY = pl.BlockSpec(memory_space=pl.ANY)
SMEM = pl.BlockSpec(memory_space=pltpu.SMEM)
VMEM = pl.BlockSpec(memory_space=pltpu.VMEM)


def rms_norm(values_in, gain):
    widened = values_in.astype(jnp.float32)
    inverse = lax.rsqrt(jnp.mean(widened * widened, axis=-1, keepdims=True) + NORM_EPS)
    return (widened * inverse * gain).astype(jnp.bfloat16)


def head_of(device, which, heads_pair):
    base = (device // 2) * heads_pair
    core = device % 2
    if which == 2:
        return base + 2
    return base + core * 3 + which


def lanes_of(head):
    return pl.ds(pl.multiple_of(head * HEAD_DIM, HEAD_DIM), HEAD_DIM)


def partner_order(devices):
    half = devices // 2
    far = list(range(half, devices))
    near = list(range(1, half))
    order = []
    for index in range(half):
        order.append(far[index])
        if index < len(near):
            order.append(near[index])
    return order


def pack_kernel(devices, heads_pair, me_ref, q_ref, k_ref, v_ref, qg_ref, kg_ref, *rest):
    x_refs, y_refs = rest[:devices], rest[devices : 2 * devices]
    q_norm, k_norm = rest[2 * devices :]
    me = me_ref[0]
    width = q_ref.shape[1]
    step = 8 * HEAD_DIM
    for src, gain, dst in ((q_ref, qg_ref, q_norm), (k_ref, kg_ref, k_norm)):
        total = jnp.zeros((TILE, HEAD_DIM), jnp.float32)
        for lane in range(0, width, HEAD_DIM):
            part = src[:, lane : lane + HEAD_DIM].astype(jnp.float32)
            total += part * part
        mean = jnp.sum(total, axis=1, keepdims=True) * (1.0 / width)
        inverse = lax.rsqrt(mean + NORM_EPS)
        for lane in range(0, width, step):
            part = src[:, lane : lane + step].astype(jnp.float32)
            dst[:, lane : lane + step] = (part * inverse * gain[:, lane : lane + step]).astype(
                jnp.bfloat16
            )
    for mask in range(devices):
        to = lax.bitwise_xor(me, mask)
        core = to % 2
        first = lanes_of(head_of(to, 0, heads_pair))
        second = lanes_of(head_of(to, 1, heads_pair))
        shared = lanes_of(head_of(to, 2, heads_pair))
        x_out, y_out = x_refs[mask], y_refs[mask]
        x_out[0:TILE] = q_norm[:, first]
        x_out[TILE : 2 * TILE] = k_norm[:, first]
        x_out[2 * TILE : 3 * TILE] = v_ref[:, first]
        half = pl.ds(pl.multiple_of(core * HALF, HALF), HALF)
        x_out[3 * TILE : 3 * TILE + HALF] = q_norm[half, shared]

        @pl.when(core == 0)
        def _():
            x_out[3 * TILE + HALF : ROWS_X] = k_norm[:, shared]

        @pl.when(core == 1)
        def _():
            x_out[3 * TILE + HALF : ROWS_X] = v_ref[:, shared]

        y_out[0:TILE] = q_norm[:, second]
        y_out[TILE : 2 * TILE] = k_norm[:, second]
        y_out[2 * TILE : 3 * TILE] = v_ref[:, second]


def pack(me, query, key, value, query_gain, key_gain, devices, heads_pair):
    shapes = [jax.ShapeDtypeStruct((ROWS_X, HEAD_DIM), jnp.bfloat16)] * devices
    shapes += [jax.ShapeDtypeStruct((ROWS_Y, HEAD_DIM), jnp.bfloat16)] * devices
    outs = pl.pallas_call(
        functools.partial(pack_kernel, devices, heads_pair),
        out_shape=shapes,
        in_specs=[SMEM] + [VMEM] * 5,
        out_specs=[VMEM] * (2 * devices),
        scratch_shapes=[pltpu.VMEM(query.shape, jnp.bfloat16)] * 2,
        compiler_params=pltpu.CompilerParams(vmem_limit_bytes=VMEM_LIMIT),
        name="norm_pack",
    )(me, query, key, value, query_gain[None, :], key_gain[None, :])
    return outs[:devices], outs[devices:]


def collect_kernel(devices, me_ref, *rest):
    x_refs, out_ref, sems = rest[:devices], rest[devices], rest[devices + 1]
    me = me_ref[0]
    copies = []
    for mask in range(devices):
        copies.append(
            pltpu.make_async_copy(
                x_refs[mask].at[pl.ds(3 * TILE + HALF, TILE)],
                out_ref.at[lax.bitwise_xor(me, mask)],
                sems.at[mask],
            )
        )
    for copy in copies:
        copy.start()
    for copy in copies:
        copy.wait()


def collect(me, x_in, devices):
    return pl.pallas_call(
        functools.partial(collect_kernel, devices),
        out_shape=jax.ShapeDtypeStruct((devices, TILE, HEAD_DIM), jnp.bfloat16),
        in_specs=[SMEM] + [ANY] * devices,
        out_specs=ANY,
        scratch_shapes=[pltpu.SemaphoreType.DMA((devices,))],
        name="collect_shared",
    )(me, *x_in)


def attend_unit(count, list_at, query_of, key_of, value_of, store):
    least = 0
    for size in UNROLLS:

        @pl.when((count > least) & (count <= size))
        def _(size=size, least=least):
            blocks = [list_at(slot) for slot in range(size)]
            query = query_of()
            keys = jnp.concatenate([key_of(block) for block in blocks], axis=0)
            scores = lax.dot_general(
                query, keys, (((1,), (1,)), ((), ())), preferred_element_type=jnp.float32
            )
            if size > least + 1:
                column = lax.broadcasted_iota(jnp.int32, scores.shape, 1)
                scores = jnp.where(column < count * TILE, scores, MASKED)
            peak = jnp.max(scores, axis=1, keepdims=True)
            weights = jnp.exp2((scores - peak) * EXP2_SCALE)
            total = jnp.sum(weights, axis=1, keepdims=True)
            values = jnp.concatenate([value_of(block) for block in blocks], axis=0)
            summed = jnp.dot(
                weights.astype(jnp.bfloat16), values, preferred_element_type=jnp.float32
            )
            store((summed / total).astype(jnp.bfloat16))

        least = size


def load_all(me, refs, held, sems):
    copies = [
        pltpu.make_async_copy(ref, held.at[lax.bitwise_xor(me, mask)], sems.at[mask])
        for mask, ref in enumerate(refs)
    ]
    for copy in copies:
        copy.start()
    return copies


def send_all(me, held, refs, sems):
    copies = [
        pltpu.make_async_copy(held.at[lax.bitwise_xor(me, mask)], ref, sems.at[mask])
        for mask, ref in enumerate(refs)
    ]
    for copy in copies:
        copy.start()
    for copy in copies:
        copy.wait()


def attend_x_kernel(
    devices, me_ref, lists_ref, counts_ref, shared_lists_ref, shared_counts_ref, *rest
):
    x_refs = rest[:devices]
    own_ref, other_ref = rest[devices : devices + 2]
    out_refs = rest[devices + 2 : 2 * devices + 2]
    held, shared, results, sems, shared_sems, out_sems = rest[2 * devices + 2 :]
    me = me_ref[0]
    core = me % 2
    copies = load_all(me, x_refs, held, sems)
    own = pltpu.make_async_copy(own_ref, shared.at[core], shared_sems.at[0])
    other = pltpu.make_async_copy(other_ref, shared.at[1 - core], shared_sems.at[1])
    own.start()
    other.start()
    for copy in copies:
        copy.wait()
    own.wait()
    other.wait()

    def step(block, carry):
        def store(values):
            results[block, 0:TILE] = values

        def store_shared(values):
            results[block, TILE : TILE + HALF] = values

        attend_unit(
            counts_ref[block],
            lambda slot: lists_ref[block * KMAX + slot],
            lambda: held[block, 0:TILE],
            lambda at: held[at, TILE : 2 * TILE],
            lambda at: held[at, 2 * TILE : 3 * TILE],
            store,
        )
        attend_unit(
            shared_counts_ref[block],
            lambda slot: shared_lists_ref[block * KMAX + slot],
            lambda: held[block, 3 * TILE : 3 * TILE + HALF],
            lambda at: shared[0, at],
            lambda at: shared[1, at],
            store_shared,
        )
        return carry

    lax.fori_loop(0, devices, step, 0)
    send_all(me, results, out_refs, out_sems)


def attend_y_kernel(devices, me_ref, lists_ref, counts_ref, *rest):
    y_refs = rest[:devices]
    out_refs = rest[devices : 2 * devices]
    held, results, sems, out_sems = rest[2 * devices :]
    me = me_ref[0]
    for copy in load_all(me, y_refs, held, sems):
        copy.wait()

    def step(block, carry):
        def store(values):
            results[block] = values

        attend_unit(
            counts_ref[block],
            lambda slot: lists_ref[block * KMAX + slot],
            lambda: held[block, 0:TILE],
            lambda at: held[at, TILE : 2 * TILE],
            lambda at: held[at, 2 * TILE : 3 * TILE],
            store,
        )
        return carry

    lax.fori_loop(0, devices, step, 0)
    send_all(me, results, out_refs, out_sems)


def attend_cost(units):
    return pl.CostEstimate(
        flops=units * 4 * 4 * TILE * TILE * HEAD_DIM,
        bytes_accessed=units * 4 * TILE * HEAD_DIM * 2,
        transcendentals=units * 4 * TILE * TILE,
    )


def attend_x(me, tables, x_in, own, other, devices):
    rows = TILE + HALF
    return pl.pallas_call(
        functools.partial(attend_x_kernel, devices),
        out_shape=[jax.ShapeDtypeStruct((rows, HEAD_DIM), jnp.bfloat16)] * devices,
        in_specs=[SMEM] * 5 + [ANY] * (devices + 2),
        out_specs=[ANY] * devices,
        scratch_shapes=[
            pltpu.VMEM((devices, ROWS_X, HEAD_DIM), jnp.bfloat16),
            pltpu.VMEM((2, devices, TILE, HEAD_DIM), jnp.bfloat16),
            pltpu.VMEM((devices, rows, HEAD_DIM), jnp.bfloat16),
            pltpu.SemaphoreType.DMA((devices,)),
            pltpu.SemaphoreType.DMA((2,)),
            pltpu.SemaphoreType.DMA((devices,)),
        ],
        compiler_params=pltpu.CompilerParams(vmem_limit_bytes=VMEM_LIMIT),
        cost_estimate=attend_cost(24),
        name="attend_x",
    )(me, *tables, *x_in, own, other)


def attend_y(me, tables, y_in, devices):
    return pl.pallas_call(
        functools.partial(attend_y_kernel, devices),
        out_shape=[jax.ShapeDtypeStruct((TILE, HEAD_DIM), jnp.bfloat16)] * devices,
        in_specs=[SMEM] * 3 + [ANY] * devices,
        out_specs=[ANY] * devices,
        scratch_shapes=[
            pltpu.VMEM((devices, ROWS_Y, HEAD_DIM), jnp.bfloat16),
            pltpu.VMEM((devices, TILE, HEAD_DIM), jnp.bfloat16),
            pltpu.SemaphoreType.DMA((devices,)),
            pltpu.SemaphoreType.DMA((devices,)),
        ],
        compiler_params=pltpu.CompilerParams(vmem_limit_bytes=VMEM_LIMIT),
        cost_estimate=attend_cost(16),
        name="attend_y",
    )(me, *tables, *y_in)


def assemble_kernel(devices, heads_pair, me_ref, *rest):
    x_refs, y_refs = rest[:devices], rest[devices : 2 * devices]
    out_ref, sems = rest[2 * devices :]
    me = me_ref[0]
    copies = []

    def add(src, dst):
        copies.append(pltpu.make_async_copy(src, dst, sems.at[len(copies)]))

    for mask in range(devices):
        source = lax.bitwise_xor(me, mask)
        core = source % 2
        first = lanes_of(head_of(source, 0, heads_pair))
        second = lanes_of(head_of(source, 1, heads_pair))
        shared = lanes_of(head_of(source, 2, heads_pair))
        half = pl.ds(pl.multiple_of(core * HALF, HALF), HALF)
        add(x_refs[mask].at[pl.ds(0, TILE)], out_ref.at[:, first])
        add(x_refs[mask].at[pl.ds(TILE, HALF)], out_ref.at[half, shared])
        add(y_refs[mask], out_ref.at[:, second])
    for copy in copies:
        copy.start()
    for copy in copies:
        copy.wait()


def assemble(me, x_back, y_back, width, devices, heads_pair):
    return pl.pallas_call(
        functools.partial(assemble_kernel, devices, heads_pair),
        out_shape=jax.ShapeDtypeStruct((TILE, width), jnp.bfloat16),
        in_specs=[SMEM] + [ANY] * (2 * devices),
        out_specs=ANY,
        scratch_shapes=[pltpu.SemaphoreType.DMA((3 * devices,))],
        name="assemble",
    )(me, *x_back, *y_back)


def exchange(parts, devices):
    arrived = [None] * devices
    arrived[0] = parts[0]
    for mask in partner_order(devices):
        arrived[mask] = lax.ppermute(
            parts[mask], "ulysses", [(index, index ^ mask) for index in range(devices)]
        )
    return arrived


def local_pairs(query, key, value, query_gain, key_gain, key_blocks, block_counts):
    devices = lax.axis_size("ulysses")
    heads_pair = 2 * HEADS // devices
    index = lax.axis_index("ulysses")
    me = index.astype(jnp.int32).reshape(1)

    def tables(which):
        head = head_of(index, which, heads_pair)
        lists = lax.dynamic_index_in_dim(key_blocks, head, 0, False).reshape(-1)
        counts = lax.dynamic_index_in_dim(block_counts, head, 0, False)
        return lists, counts

    x_out, y_out = pack(me, query, key, value, query_gain, key_gain, devices, heads_pair)
    x_in = exchange(x_out, devices)
    y_in = exchange(y_out, devices)
    own = collect(me, x_in, devices)
    other = lax.ppermute(own, "ulysses", [(at, at ^ 1) for at in range(devices)])
    x_results = attend_x(me, tables(0) + tables(2), x_in, own, other, devices)
    x_back = exchange(x_results, devices)
    y_results = attend_y(me, tables(1), y_in, devices)
    y_back = exchange(y_results, devices)
    return assemble(me, x_back, y_back, query.shape[1], devices, heads_pair)


def pick_group():
    for group_size in (8, 4, 2, 1):
        return group_size
    return 1


def local_any(query, key, value, query_gain, key_gain, key_blocks, block_counts):
    devices = lax.axis_size("ulysses")
    my_index = lax.axis_index("ulysses")
    tok_dev = query.shape[0]
    blocks = tok_dev * devices // TILE
    per_device = HEADS * tok_dev // TILE
    unit_total = HEADS * blocks
    softmax_scale = HEAD_DIM ** (-0.5)
    q_norm = rms_norm(query, query_gain)
    k_norm = rms_norm(key, key_gain)
    marks_all = jnp.arange(devices + 1, dtype=jnp.int32)
    bounds = marks_all * per_device
    span_heads = min(HEADS, (per_device + blocks - 2) // blocks + 1)
    first_head = bounds[:-1] // blocks
    owner_heads = jnp.minimum(
        first_head[:, None] + jnp.arange(span_heads, dtype=jnp.int32)[None, :], HEADS - 1
    )
    packed = (
        jnp.stack([q_norm, k_norm, value], axis=0)
        .reshape(3, tok_dev, HEADS, HEAD_DIM)
        .transpose(2, 0, 1, 3)
    )
    outgoing = (
        packed[owner_heads.T]
        .transpose(0, 2, 1, 3, 4)
        .reshape(span_heads * 3, devices * tok_dev, HEAD_DIM)
    )
    arrived = lax.all_to_all(outgoing, "ulysses", split_axis=1, concat_axis=1, tiled=True)
    resident = arrived.reshape(span_heads, 3, blocks, TILE, HEAD_DIM)
    unit_start = bounds[my_index]
    unit_count = bounds[my_index + 1] - unit_start
    base_head = unit_start // blocks
    group_size = pick_group()
    results = jnp.zeros((span_heads, blocks, TILE, HEAD_DIM), jnp.bfloat16)

    def attend_group(step_index, results):
        local_units = step_index * group_size + jnp.arange(group_size, dtype=jnp.int32)
        unit_live = local_units < unit_count
        unit_ids = jnp.minimum(unit_start + local_units, unit_total - 1)
        unit_heads = unit_ids // blocks
        qblock = unit_ids % blocks
        unit_slots = jnp.clip(unit_heads - base_head, 0, span_heads - 1)
        key_lists = key_blocks[unit_heads, qblock]
        live_count = block_counts[unit_heads, qblock]
        query_matrix = resident[unit_slots, 0, qblock]
        key_panels = resident[unit_slots[:, None], 1, key_lists]
        value_panels = resident[unit_slots[:, None], 2, key_lists]
        logit_matrix = (
            jnp.einsum(
                "gqd,gjkd->gqjk", query_matrix, key_panels, preferred_element_type=jnp.float32
            )
            * softmax_scale
        )
        live_mask = (jnp.arange(KMAX, dtype=jnp.int32)[None, :] < live_count[:, None])[
            :, None, :, None
        ]
        logit_matrix = jnp.where(live_mask, logit_matrix, MASKED)
        row_peak = jnp.max(logit_matrix, axis=(2, 3), keepdims=True)
        weights = jnp.where(live_mask, jnp.exp(logit_matrix - row_peak), 0.0)
        row_denominator = jnp.sum(weights, axis=(2, 3))
        summed = jnp.einsum(
            "gqjk,gjkd->gqd",
            weights.astype(jnp.bfloat16),
            value_panels,
            preferred_element_type=jnp.float32,
        )
        combined = (summed / row_denominator[:, :, None]).astype(jnp.bfloat16)
        write_slots = jnp.where(unit_live, unit_slots, span_heads)
        return results.at[write_slots, qblock].set(combined, mode="drop")

    step_total = (unit_count + group_size - 1) // group_size
    results = lax.fori_loop(0, step_total, attend_group, results)
    leaving = results.reshape(span_heads, blocks * TILE, HEAD_DIM)
    returned = lax.all_to_all(leaving, "ulysses", split_axis=1, concat_axis=0, tiled=True)
    head_range = jnp.arange(HEADS, dtype=jnp.int32)
    selector = (owner_heads.reshape(-1)[None, :] == head_range[:, None]).astype(jnp.bfloat16)
    gathered = jnp.einsum("hs,std->thd", selector, returned, preferred_element_type=jnp.float32)
    return gathered.astype(jnp.bfloat16).reshape(tok_dev, HEADS * HEAD_DIM)


def local(query, *rest):
    devices = lax.axis_size("ulysses")
    power_of_two = devices & (devices - 1) == 0
    five_a_pair = devices % 2 == 0 and devices * 5 == HEADS * 2
    if power_of_two and five_a_pair and query.shape[0] == TILE:
        return local_pairs(query, *rest)
    return local_any(query, *rest)


def solution(mesh):
    in_specs = (
        P(("parts", "ulysses"), None),
        P(("parts", "ulysses"), None),
        P(("parts", "ulysses"), None),
        P(),
        P(),
        P("parts", None, None),
        P("parts", None),
    )
    out_specs = P(("parts", "ulysses"), None)
    return jax.shard_map(local, mesh=mesh, in_specs=in_specs, out_specs=out_specs, check_vma=False)
```

```python
import functools
import math

import jax
import jax.numpy as jnp
from jax import lax
from jax.experimental import pallas as pl
from jax.experimental.pallas import tpu as pltpu
from jax.sharding import PartitionSpec as P

HEADS = 40
HEAD_DIM = 128
TILE = 128
KMAX = 12
HALF = TILE // 2

NORM_EPS = 1e-06
MASKED = -1e30
EXP2_SCALE = HEAD_DIM ** (-0.5) * math.log2(math.e)
UNROLLS = (1, 2, 3, 4, 6, 8, 10, 12)
VMEM_LIMIT = 12 * 1024 * 1024

ROWS_X = 3 * TILE + HALF + TILE
ROWS_Y = 3 * TILE

IN_FLIGHT = 5

ANY = pl.BlockSpec(memory_space=pl.ANY)
SMEM = pl.BlockSpec(memory_space=pltpu.SMEM)
VMEM = pl.BlockSpec(memory_space=pltpu.VMEM)


def rms_norm(values_in, gain):
    widened = values_in.astype(jnp.float32)
    inverse = lax.rsqrt(jnp.mean(widened * widened, axis=-1, keepdims=True) + NORM_EPS)
    return (widened * inverse * gain).astype(jnp.bfloat16)


def head_of(device, which, heads_pair):
    base = (device // 2) * heads_pair
    core = device % 2
    if which == 2:
        return base + 2
    return base + core * 3 + which


def lanes_of(head):
    return pl.ds(pl.multiple_of(head * HEAD_DIM, HEAD_DIM), HEAD_DIM)


def masks_of(devices):
    half = devices // 2
    far = list(range(half, devices))
    near = list(range(1, half))
    order = [0]
    for index in range(half):
        order.append(far[index])
        if index < len(near):
            order.append(near[index])
    return order


def pack_kernel(devices, heads_pair, me_ref, q_ref, k_ref, v_ref, qg_ref, kg_ref, *rest):
    x_refs, y_refs = rest[:devices], rest[devices : 2 * devices]
    q_norm, k_norm = rest[2 * devices :]
    me = me_ref[0]
    width = q_ref.shape[1]
    step = 8 * HEAD_DIM
    for src, gain, dst in ((q_ref, qg_ref, q_norm), (k_ref, kg_ref, k_norm)):
        total = jnp.zeros((TILE, HEAD_DIM), jnp.float32)
        for lane in range(0, width, HEAD_DIM):
            part = src[:, lane : lane + HEAD_DIM].astype(jnp.float32)
            total += part * part
        mean = jnp.sum(total, axis=1, keepdims=True) * (1.0 / width)
        inverse = lax.rsqrt(mean + NORM_EPS)
        for lane in range(0, width, step):
            part = src[:, lane : lane + step].astype(jnp.float32)
            dst[:, lane : lane + step] = (part * inverse * gain[:, lane : lane + step]).astype(
                jnp.bfloat16
            )
    for mask, x_out, y_out in zip(masks_of(devices), x_refs, y_refs):
        to = lax.bitwise_xor(me, mask)
        core = to % 2
        first = lanes_of(head_of(to, 0, heads_pair))
        second = lanes_of(head_of(to, 1, heads_pair))
        shared = lanes_of(head_of(to, 2, heads_pair))
        x_out[0:TILE] = q_norm[:, first]
        x_out[TILE : 2 * TILE] = k_norm[:, first]
        x_out[2 * TILE : 3 * TILE] = v_ref[:, first]
        half = pl.ds(pl.multiple_of(core * HALF, HALF), HALF)
        x_out[3 * TILE : 3 * TILE + HALF] = q_norm[half, shared]

        @pl.when(core == 0)
        def _():
            x_out[3 * TILE + HALF : ROWS_X] = k_norm[:, shared]

        @pl.when(core == 1)
        def _():
            x_out[3 * TILE + HALF : ROWS_X] = v_ref[:, shared]

        y_out[0:TILE] = q_norm[:, second]
        y_out[TILE : 2 * TILE] = k_norm[:, second]
        y_out[2 * TILE : 3 * TILE] = v_ref[:, second]


def pack(me, query, key, value, query_gain, key_gain, devices, heads_pair):
    shapes = [jax.ShapeDtypeStruct((ROWS_X, HEAD_DIM), jnp.bfloat16)] * devices
    shapes += [jax.ShapeDtypeStruct((ROWS_Y, HEAD_DIM), jnp.bfloat16)] * devices
    outs = pl.pallas_call(
        functools.partial(pack_kernel, devices, heads_pair),
        out_shape=shapes,
        in_specs=[SMEM] + [VMEM] * 5,
        out_specs=[VMEM] * (2 * devices),
        scratch_shapes=[pltpu.VMEM(query.shape, jnp.bfloat16)] * 2,
        compiler_params=pltpu.CompilerParams(vmem_limit_bytes=VMEM_LIMIT),
        name="norm_pack",
    )(me, query, key, value, query_gain[None, :], key_gain[None, :])
    return outs[:devices], outs[devices:]


def collect_kernel(devices, me_ref, *rest):
    x_refs, out_ref = rest[:devices], rest[devices]
    me = me_ref[0]
    for mask, x_ref in zip(masks_of(devices), x_refs):
        out_ref[lax.bitwise_xor(me, mask)] = x_ref[3 * TILE + HALF : ROWS_X]


def collect(me, x_in, devices):
    return pl.pallas_call(
        functools.partial(collect_kernel, devices),
        out_shape=jax.ShapeDtypeStruct((devices, TILE, HEAD_DIM), jnp.bfloat16),
        in_specs=[SMEM] + [VMEM] * devices,
        out_specs=VMEM,
        compiler_params=pltpu.CompilerParams(vmem_limit_bytes=VMEM_LIMIT),
        name="collect_shared",
    )(me, *x_in)


def attend_unit(count, list_at, query_of, key_of, value_of, store):
    least = 0
    for size in UNROLLS:

        @pl.when((count > least) & (count <= size))
        def _(size=size, least=least):
            blocks = [list_at(slot) for slot in range(size)]
            query = query_of()
            keys = jnp.concatenate([key_of(block) for block in blocks], axis=0)
            scores = lax.dot_general(
                query, keys, (((1,), (1,)), ((), ())), preferred_element_type=jnp.float32
            )
            if size > least + 1:
                column = lax.broadcasted_iota(jnp.int32, scores.shape, 1)
                scores = jnp.where(column < count * TILE, scores, MASKED)
            peak = jnp.max(scores, axis=1, keepdims=True)
            weights = jnp.exp2((scores - peak) * EXP2_SCALE)
            total = jnp.sum(weights, axis=1, keepdims=True)
            values = jnp.concatenate([value_of(block) for block in blocks], axis=0)
            summed = jnp.dot(
                weights.astype(jnp.bfloat16), values, preferred_element_type=jnp.float32
            )
            store((summed / total).astype(jnp.bfloat16))

        least = size


def load_all(me, refs, held, sems):
    copies = [
        pltpu.make_async_copy(ref, held.at[lax.bitwise_xor(me, mask)], sems.at[mask])
        for mask, ref in zip(masks_of(len(refs)), refs)
    ]
    for copy in copies:
        copy.start()
    return copies


def send_all(me, held, refs, sems):
    copies = [
        pltpu.make_async_copy(held.at[lax.bitwise_xor(me, mask)], ref, sems.at[mask])
        for mask, ref in zip(masks_of(len(refs)), refs)
    ]
    for copy in copies:
        copy.start()
    for copy in copies:
        copy.wait()


def attend_x_kernel(
    devices, me_ref, lists_ref, counts_ref, shared_lists_ref, shared_counts_ref, *rest
):
    x_refs = rest[:devices]
    own_ref, other_ref = rest[devices : devices + 2]
    out_refs = rest[devices + 2 : 2 * devices + 2]
    held, shared, results, sems, shared_sems, out_sems = rest[2 * devices + 2 :]
    me = me_ref[0]
    core = me % 2
    copies = load_all(me, x_refs, held, sems)
    own = pltpu.make_async_copy(own_ref, shared.at[core], shared_sems.at[0])
    other = pltpu.make_async_copy(other_ref, shared.at[1 - core], shared_sems.at[1])
    own.start()
    other.start()
    for copy in copies:
        copy.wait()
    own.wait()
    other.wait()

    def step(block, carry):
        def store(values):
            results[block, 0:TILE] = values

        def store_shared(values):
            results[block, TILE : TILE + HALF] = values

        attend_unit(
            counts_ref[block],
            lambda slot: lists_ref[block * KMAX + slot],
            lambda: held[block, 0:TILE],
            lambda at: held[at, TILE : 2 * TILE],
            lambda at: held[at, 2 * TILE : 3 * TILE],
            store,
        )
        attend_unit(
            shared_counts_ref[block],
            lambda slot: shared_lists_ref[block * KMAX + slot],
            lambda: held[block, 3 * TILE : 3 * TILE + HALF],
            lambda at: shared[0, at],
            lambda at: shared[1, at],
            store_shared,
        )
        return carry

    lax.fori_loop(0, devices, step, 0)
    send_all(me, results, out_refs, out_sems)


def attend_y_kernel(devices, me_ref, lists_ref, counts_ref, *rest):
    y_refs = rest[:devices]
    out_refs = rest[devices : 2 * devices]
    held, results, sems, out_sems = rest[2 * devices :]
    me = me_ref[0]
    for copy in load_all(me, y_refs, held, sems):
        copy.wait()

    def step(block, carry):
        def store(values):
            results[block] = values

        attend_unit(
            counts_ref[block],
            lambda slot: lists_ref[block * KMAX + slot],
            lambda: held[block, 0:TILE],
            lambda at: held[at, TILE : 2 * TILE],
            lambda at: held[at, 2 * TILE : 3 * TILE],
            store,
        )
        return carry

    lax.fori_loop(0, devices, step, 0)
    send_all(me, results, out_refs, out_sems)


def attend_cost(units):
    return pl.CostEstimate(
        flops=units * 4 * 4 * TILE * TILE * HEAD_DIM,
        bytes_accessed=units * 4 * TILE * HEAD_DIM * 2,
        transcendentals=units * 4 * TILE * TILE,
    )


def attend_x(me, tables, x_in, own, other, devices):
    rows = TILE + HALF
    return pl.pallas_call(
        functools.partial(attend_x_kernel, devices),
        out_shape=[jax.ShapeDtypeStruct((rows, HEAD_DIM), jnp.bfloat16)] * devices,
        in_specs=[SMEM] * 5 + [ANY] * (devices + 2),
        out_specs=[ANY] * devices,
        scratch_shapes=[
            pltpu.VMEM((devices, ROWS_X, HEAD_DIM), jnp.bfloat16),
            pltpu.VMEM((2, devices, TILE, HEAD_DIM), jnp.bfloat16),
            pltpu.VMEM((devices, rows, HEAD_DIM), jnp.bfloat16),
            pltpu.SemaphoreType.DMA((devices,)),
            pltpu.SemaphoreType.DMA((2,)),
            pltpu.SemaphoreType.DMA((devices,)),
        ],
        compiler_params=pltpu.CompilerParams(vmem_limit_bytes=VMEM_LIMIT),
        cost_estimate=attend_cost(24),
        name="attend_x",
    )(me, *tables, *x_in, own, other)


def attend_y(me, tables, y_in, devices):
    return pl.pallas_call(
        functools.partial(attend_y_kernel, devices),
        out_shape=[jax.ShapeDtypeStruct((TILE, HEAD_DIM), jnp.bfloat16)] * devices,
        in_specs=[SMEM] * 3 + [ANY] * devices,
        out_specs=[ANY] * devices,
        scratch_shapes=[
            pltpu.VMEM((devices, ROWS_Y, HEAD_DIM), jnp.bfloat16),
            pltpu.VMEM((devices, TILE, HEAD_DIM), jnp.bfloat16),
            pltpu.SemaphoreType.DMA((devices,)),
            pltpu.SemaphoreType.DMA((devices,)),
        ],
        compiler_params=pltpu.CompilerParams(vmem_limit_bytes=VMEM_LIMIT),
        cost_estimate=attend_cost(16),
        name="attend_y",
    )(me, *tables, *y_in)


def assemble_kernel(devices, heads_pair, me_ref, *rest):
    x_refs, y_refs = rest[:devices], rest[devices : 2 * devices]
    out_ref, sems = rest[2 * devices :]
    me = me_ref[0]
    copies = []

    def add(src, dst):
        copies.append(pltpu.make_async_copy(src, dst, sems.at[len(copies)]))

    for mask, x_ref, y_ref in zip(masks_of(devices), x_refs, y_refs):
        source = lax.bitwise_xor(me, mask)
        core = source % 2
        first = lanes_of(head_of(source, 0, heads_pair))
        second = lanes_of(head_of(source, 1, heads_pair))
        shared = lanes_of(head_of(source, 2, heads_pair))
        half = pl.ds(pl.multiple_of(core * HALF, HALF), HALF)
        add(x_ref.at[pl.ds(0, TILE)], out_ref.at[:, first])
        add(x_ref.at[pl.ds(TILE, HALF)], out_ref.at[half, shared])
        add(y_ref, out_ref.at[:, second])
    for copy in copies:
        copy.start()
    for copy in copies:
        copy.wait()


def assemble(me, x_back, y_back, width, devices, heads_pair):
    return pl.pallas_call(
        functools.partial(assemble_kernel, devices, heads_pair),
        out_shape=jax.ShapeDtypeStruct((TILE, width), jnp.bfloat16),
        in_specs=[SMEM] + [VMEM] * (2 * devices),
        out_specs=ANY,
        scratch_shapes=[pltpu.SemaphoreType.DMA((3 * devices,))],
        compiler_params=pltpu.CompilerParams(vmem_limit_bytes=VMEM_LIMIT),
        name="assemble",
    )(me, *x_back, *y_back)


def exchange(parts, devices, masks):
    return [
        part
        if mask == 0
        else lax.ppermute(part, "ulysses", [(index, index ^ mask) for index in range(devices)])
        for mask, part in zip(masks, parts)
    ]


def local_pairs(query, key, value, query_gain, key_gain, key_blocks, block_counts):
    devices = lax.axis_size("ulysses")
    heads_pair = 2 * HEADS // devices
    index = lax.axis_index("ulysses")
    me = index.astype(jnp.int32).reshape(1)

    def tables(which):
        head = head_of(index, which, heads_pair)
        lists = lax.dynamic_index_in_dim(key_blocks, head, 0, False).reshape(-1)
        counts = lax.dynamic_index_in_dim(block_counts, head, 0, False)
        return lists, counts

    x_out, y_out = pack(me, query, key, value, query_gain, key_gain, devices, heads_pair)
    masks = masks_of(devices)
    x_in = exchange(x_out, devices, masks)
    own = collect(me, x_in, devices)
    other = lax.ppermute(own, "ulysses", [(at, at ^ 1) for at in range(devices)])
    far = [place for place, mask in enumerate(masks) if mask >= devices // 2]
    early = far[:IN_FLIGHT - 1]
    late = [place for place in range(1, devices) if place not in early]
    y_in = [y_out[0]] + [None] * (devices - 1)
    y_early = exchange([y_out[at] for at in early], devices, [masks[at] for at in early])
    x_results = attend_x(me, tables(0) + tables(2), x_in, own, other, devices)
    y_late, x_results = lax.optimization_barrier(([y_out[at] for at in late], x_results))
    y_late = exchange(y_late, devices, [masks[at] for at in late])
    for at, part in zip(early + late, y_early + y_late):
        y_in[at] = part
    x_back = exchange(x_results, devices, masks)
    y_results = attend_y(me, tables(1), y_in, devices)
    y_back = exchange(y_results, devices, masks)
    return assemble(me, x_back, y_back, query.shape[1], devices, heads_pair)


def pick_group():
    for group_size in (8, 4, 2, 1):
        return group_size
    return 1


def local_any(query, key, value, query_gain, key_gain, key_blocks, block_counts):
    devices = lax.axis_size("ulysses")
    my_index = lax.axis_index("ulysses")
    tok_dev = query.shape[0]
    blocks = tok_dev * devices // TILE
    per_device = HEADS * tok_dev // TILE
    unit_total = HEADS * blocks
    softmax_scale = HEAD_DIM ** (-0.5)
    q_norm = rms_norm(query, query_gain)
    k_norm = rms_norm(key, key_gain)
    marks_all = jnp.arange(devices + 1, dtype=jnp.int32)
    bounds = marks_all * per_device
    span_heads = min(HEADS, (per_device + blocks - 2) // blocks + 1)
    first_head = bounds[:-1] // blocks
    owner_heads = jnp.minimum(
        first_head[:, None] + jnp.arange(span_heads, dtype=jnp.int32)[None, :], HEADS - 1
    )
    packed = (
        jnp.stack([q_norm, k_norm, value], axis=0)
        .reshape(3, tok_dev, HEADS, HEAD_DIM)
        .transpose(2, 0, 1, 3)
    )
    outgoing = (
        packed[owner_heads.T]
        .transpose(0, 2, 1, 3, 4)
        .reshape(span_heads * 3, devices * tok_dev, HEAD_DIM)
    )
    arrived = lax.all_to_all(outgoing, "ulysses", split_axis=1, concat_axis=1, tiled=True)
    resident = arrived.reshape(span_heads, 3, blocks, TILE, HEAD_DIM)
    unit_start = bounds[my_index]
    unit_count = bounds[my_index + 1] - unit_start
    base_head = unit_start // blocks
    group_size = pick_group()
    results = jnp.zeros((span_heads, blocks, TILE, HEAD_DIM), jnp.bfloat16)

    def attend_group(step_index, results):
        local_units = step_index * group_size + jnp.arange(group_size, dtype=jnp.int32)
        unit_live = local_units < unit_count
        unit_ids = jnp.minimum(unit_start + local_units, unit_total - 1)
        unit_heads = unit_ids // blocks
        qblock = unit_ids % blocks
        unit_slots = jnp.clip(unit_heads - base_head, 0, span_heads - 1)
        key_lists = key_blocks[unit_heads, qblock]
        live_count = block_counts[unit_heads, qblock]
        query_matrix = resident[unit_slots, 0, qblock]
        key_panels = resident[unit_slots[:, None], 1, key_lists]
        value_panels = resident[unit_slots[:, None], 2, key_lists]
        logit_matrix = (
            jnp.einsum(
                "gqd,gjkd->gqjk", query_matrix, key_panels, preferred_element_type=jnp.float32
            )
            * softmax_scale
        )
        live_mask = (jnp.arange(KMAX, dtype=jnp.int32)[None, :] < live_count[:, None])[
            :, None, :, None
        ]
        logit_matrix = jnp.where(live_mask, logit_matrix, MASKED)
        row_peak = jnp.max(logit_matrix, axis=(2, 3), keepdims=True)
        weights = jnp.where(live_mask, jnp.exp(logit_matrix - row_peak), 0.0)
        row_denominator = jnp.sum(weights, axis=(2, 3))
        summed = jnp.einsum(
            "gqjk,gjkd->gqd",
            weights.astype(jnp.bfloat16),
            value_panels,
            preferred_element_type=jnp.float32,
        )
        combined = (summed / row_denominator[:, :, None]).astype(jnp.bfloat16)
        write_slots = jnp.where(unit_live, unit_slots, span_heads)
        return results.at[write_slots, qblock].set(combined, mode="drop")

    step_total = (unit_count + group_size - 1) // group_size
    results = lax.fori_loop(0, step_total, attend_group, results)
    leaving = results.reshape(span_heads, blocks * TILE, HEAD_DIM)
    returned = lax.all_to_all(leaving, "ulysses", split_axis=1, concat_axis=0, tiled=True)
    head_range = jnp.arange(HEADS, dtype=jnp.int32)
    selector = (owner_heads.reshape(-1)[None, :] == head_range[:, None]).astype(jnp.bfloat16)
    gathered = jnp.einsum("hs,std->thd", selector, returned, preferred_element_type=jnp.float32)
    return gathered.astype(jnp.bfloat16).reshape(tok_dev, HEADS * HEAD_DIM)


def local(query, *rest):
    devices = lax.axis_size("ulysses")
    power_of_two = devices & (devices - 1) == 0
    five_a_pair = devices % 2 == 0 and devices * 5 == HEADS * 2
    if power_of_two and five_a_pair and query.shape[0] == TILE:
        return local_pairs(query, *rest)
    return local_any(query, *rest)


def solution(mesh):
    in_specs = (
        P(("parts", "ulysses"), None),
        P(("parts", "ulysses"), None),
        P(("parts", "ulysses"), None),
        P(),
        P(),
        P("parts", None, None),
        P("parts", None),
    )
    out_specs = P(("parts", "ulysses"), None)
    return jax.shard_map(local, mesh=mesh, in_specs=in_specs, out_specs=out_specs, check_vma=False)
```

```python
import functools
import math

import jax
import jax.numpy as jnp
from jax import lax
from jax.experimental import pallas as pl
from jax.experimental.pallas import tpu as pltpu
from jax.sharding import PartitionSpec as P

HEADS = 40
HEAD_DIM = 128
TILE = 128
KMAX = 12
HALF = TILE // 2

NORM_EPS = 1e-06
MASKED = -1e30
EXP2_SCALE = HEAD_DIM ** (-0.5) * math.log2(math.e)
SIZES = (2, 4, 6, 8, 10, 12)
TOGETHER = 4
VMEM_LIMIT = 12 * 1024 * 1024

HEAD_ROWS = 3 * TILE
SHARED_Q = 2 * HEAD_ROWS
SHARED_KV = SHARED_Q + HALF
ROWS = SHARED_KV + TILE
BACK_ROWS = 2 * TILE + HALF

HBM = pl.BlockSpec(memory_space=pltpu.HBM)
SMEM = pl.BlockSpec(memory_space=pltpu.SMEM)
VMEM = pl.BlockSpec(memory_space=pltpu.VMEM)
PARAMS = pltpu.CompilerParams(vmem_limit_bytes=VMEM_LIMIT)


def rms_norm(values_in, gain):
    widened = values_in.astype(jnp.float32)
    inverse = lax.rsqrt(jnp.mean(widened * widened, axis=-1, keepdims=True) + NORM_EPS)
    return (widened * inverse * gain).astype(jnp.bfloat16)


def head_of(device, which, heads_pair):
    base = (device // 2) * heads_pair
    core = device % 2
    if which == 2:
        return base + 2
    return base + core * 3 + which


def lanes_of(head):
    return pl.ds(pl.multiple_of(head * HEAD_DIM, HEAD_DIM), HEAD_DIM)


def alternate(far, near):
    order = []
    for index in range(max(len(far), len(near))):
        order += far[index : index + 1] + near[index : index + 1]
    return order


def partners(devices):
    half = devices // 2
    far = list(range(devices - 1, half - 1, -1))
    near = list(range(half // 2, half)) + list(range(1, half // 2))
    return far, near


def pack_kernel(masks, heads_pair, me_ref, q_hbm, k_hbm, v_hbm, qg_hbm, kg_hbm, *rest):
    out_refs = rest[: len(masks)]
    q_ref, k_ref, v_ref, qg_ref, kg_ref, q_norm, k_norm, sems = rest[len(masks) :]
    me = me_ref[0]
    loads = [
        pltpu.make_async_copy(src, dst, sems.at[at])
        for at, (src, dst) in enumerate(
            (
                (qg_hbm, qg_ref),
                (kg_hbm, kg_ref),
                (q_hbm, q_ref),
                (k_hbm, k_ref),
                (v_hbm, v_ref),
            )
        )
    ]
    for load in loads:
        load.start()
    loads[0].wait()
    loads[1].wait()
    width = q_ref.shape[1]
    step = 8 * HEAD_DIM
    for load, src, gain, dst in (
        (loads[2], q_ref, qg_ref, q_norm),
        (loads[3], k_ref, kg_ref, k_norm),
    ):
        load.wait()
        total = jnp.zeros((TILE, HEAD_DIM), jnp.float32)
        for lane in range(0, width, HEAD_DIM):
            part = src[:, lane : lane + HEAD_DIM].astype(jnp.float32)
            total += part * part
        mean = jnp.sum(total, axis=1, keepdims=True) * (1.0 / width)
        inverse = lax.rsqrt(mean + NORM_EPS)
        for lane in range(0, width, step):
            part = src[:, lane : lane + step].astype(jnp.float32)
            dst[:, lane : lane + step] = (part * inverse * gain[:, lane : lane + step]).astype(
                jnp.bfloat16
            )
    loads[4].wait()
    for mask, out in zip(masks, out_refs):
        to = lax.bitwise_xor(me, mask)
        core = to % 2
        for which in range(2):
            lanes = lanes_of(head_of(to, which, heads_pair))
            row = which * HEAD_ROWS
            out[row : row + TILE] = q_norm[:, lanes]
            out[row + TILE : row + 2 * TILE] = k_norm[:, lanes]
            out[row + 2 * TILE : row + 3 * TILE] = v_ref[:, lanes]
        lanes = lanes_of(head_of(to, 2, heads_pair))
        half = pl.ds(pl.multiple_of(core * HALF, HALF), HALF)
        out[SHARED_Q:SHARED_KV] = q_norm[half, lanes]

        @pl.when(core == 0)
        def _(out=out, lanes=lanes):
            out[SHARED_KV:ROWS] = k_norm[:, lanes]

        @pl.when(core == 1)
        def _(out=out, lanes=lanes):
            out[SHARED_KV:ROWS] = v_ref[:, lanes]


def pack(me, query, key, value, query_gain, key_gain, masks, heads_pair):
    gain = pltpu.VMEM((1, query.shape[1]), jnp.float32)
    return pl.pallas_call(
        functools.partial(pack_kernel, masks, heads_pair),
        out_shape=[jax.ShapeDtypeStruct((ROWS, HEAD_DIM), jnp.bfloat16)] * len(masks),
        in_specs=[SMEM] + [HBM] * 5,
        out_specs=[VMEM] * len(masks),
        scratch_shapes=[pltpu.VMEM(query.shape, jnp.bfloat16)] * 3
        + [gain] * 2
        + [pltpu.VMEM(query.shape, jnp.bfloat16)] * 2
        + [pltpu.SemaphoreType.DMA((5,))],
        compiler_params=PARAMS,
        name="norm_pack",
    )(me, query, key, value, query_gain[None, :], key_gain[None, :])


def collect_kernel(masks, me_ref, *rest):
    in_refs, out_ref = rest[: len(masks)], rest[len(masks)]
    me = me_ref[0]
    for mask, ref in zip(masks, in_refs):
        out_ref[lax.bitwise_xor(me, mask)] = ref[SHARED_KV:ROWS]


def collect(me, arrived, masks):
    return pl.pallas_call(
        functools.partial(collect_kernel, masks),
        out_shape=jax.ShapeDtypeStruct((len(masks), TILE, HEAD_DIM), jnp.bfloat16),
        in_specs=[SMEM] + [VMEM] * len(masks),
        out_specs=VMEM,
        compiler_params=PARAMS,
        name="collect_shared",
    )(me, *arrived)


def attend_together(counts, list_at, query_of, key_of, value_of, store):
    longest = functools.reduce(jnp.maximum, counts)
    least = 0
    for size in SIZES:

        @pl.when((longest > least) & (longest <= size))
        def _(size=size):
            column = lax.broadcasted_iota(jnp.int32, (1, size * TILE), 1)
            units = range(len(counts))
            picked = [[list_at(unit, slot) for slot in range(size)] for unit in units]
            scores = []
            for unit in units:
                keys = jnp.concatenate([key_of(block) for block in picked[unit]], axis=0)
                scores.append(
                    lax.dot_general(
                        query_of(unit),
                        keys,
                        (((1,), (1,)), ((), ())),
                        preferred_element_type=jnp.float32,
                    )
                    + jnp.where(column < counts[unit] * TILE, 0.0, MASKED)
                )
            weights, totals = [], []
            for unit in units:
                peak = jnp.max(scores[unit], axis=1, keepdims=True)
                wide = jnp.exp2((scores[unit] - peak) * EXP2_SCALE)
                totals.append(jnp.sum(wide, axis=1, keepdims=True))
                weights.append(wide.astype(jnp.bfloat16))
            summed = []
            for unit in units:
                values = jnp.concatenate([value_of(block) for block in picked[unit]], axis=0)
                summed.append(
                    jnp.dot(weights[unit], values, preferred_element_type=jnp.float32)
                )
            for unit in units:
                store(unit, (summed[unit] / totals[unit]).astype(jnp.bfloat16))

        least = size


def attend_own(me, masks, head, lists_ref, counts_ref, held, store):
    blocks = [lax.bitwise_xor(me, mask) for mask in masks]
    devices = held.shape[0]
    row = head * HEAD_ROWS
    rows = [pl.ds(pl.multiple_of(row + part * TILE, TILE), TILE) for part in range(3)]
    attend_together(
        [counts_ref[head * devices + block] for block in blocks],
        lambda unit, slot: lists_ref[(head * devices + blocks[unit]) * KMAX + slot],
        lambda unit: held[blocks[unit], rows[0]],
        lambda at: held[at, rows[1]],
        lambda at: held[at, rows[2]],
        store,
    )


def attend_shared(me, masks, lists_ref, counts_ref, held, shared, store):
    blocks = [lax.bitwise_xor(me, mask) for mask in masks]
    devices = held.shape[0]
    attend_together(
        [counts_ref[2 * devices + block] for block in blocks],
        lambda unit, slot: lists_ref[(2 * devices + blocks[unit]) * KMAX + slot],
        lambda unit: held[blocks[unit], SHARED_Q:SHARED_KV],
        lambda at: shared[0, at],
        lambda at: shared[1, at],
        store,
    )


def attend_first_kernel(masks, first, me_ref, lists_ref, counts_ref, *rest):
    in_refs = rest[: len(masks)]
    held, results = rest[len(masks) :]
    me = me_ref[0]
    for mask, ref in zip(masks, in_refs):
        held[lax.bitwise_xor(me, mask)] = ref[0:SHARED_KV]

    def step(head, carry):
        def store(unit, values):
            results[unit, pl.ds(pl.multiple_of(head * TILE, TILE), TILE)] = values

        attend_own(me, first, head, lists_ref, counts_ref, held, store)
        return carry

    lax.fori_loop(0, 2, step, 0)


def attend_first(me, tables, arrived, masks, first):
    devices = len(masks)
    return pl.pallas_call(
        functools.partial(attend_first_kernel, masks, first),
        out_shape=[
            jax.ShapeDtypeStruct((devices, SHARED_KV, HEAD_DIM), jnp.bfloat16),
            jax.ShapeDtypeStruct((len(first), 2 * TILE, HEAD_DIM), jnp.bfloat16),
        ],
        in_specs=[SMEM] * 3 + [VMEM] * devices,
        out_specs=[VMEM] * 2,
        compiler_params=PARAMS,
        cost_estimate=attend_cost(2 * len(first)),
        name="attend_first",
    )(me, *tables, *arrived)


def attend_second_kernel(
    first, me_ref, lists_ref, counts_ref, held, own_ref, other_ref, begun, shared, *out_refs
):
    me = me_ref[0]
    core = me % 2
    shared[core] = own_ref[...]
    shared[1 - core] = other_ref[...]
    for unit, out in enumerate(out_refs):
        out[0 : 2 * TILE] = begun[unit]

    def store(unit, values):
        out_refs[unit][2 * TILE : BACK_ROWS] = values

    attend_shared(me, first, lists_ref, counts_ref, held, shared, store)


def attend_second(me, tables, held, own, other, begun, first):
    devices = held.shape[0]
    back = jax.ShapeDtypeStruct((BACK_ROWS, HEAD_DIM), jnp.bfloat16)
    outs = pl.pallas_call(
        functools.partial(attend_second_kernel, first),
        out_shape=[jax.ShapeDtypeStruct((2, devices, TILE, HEAD_DIM), jnp.bfloat16)]
        + [back] * len(first),
        in_specs=[SMEM] * 3 + [VMEM] * 4,
        out_specs=[VMEM] * (1 + len(first)),
        compiler_params=PARAMS,
        cost_estimate=attend_cost(len(first)),
        name="attend_second",
    )(me, *tables, held, own, other, begun)
    return outs[0], list(outs[1:])


def attend_rest_kernel(masks, me_ref, lists_ref, counts_ref, held, shared, *rest):
    out_refs, results = rest[: len(masks)], rest[len(masks)]
    me = me_ref[0]
    groups = len(masks) // TOGETHER

    def own_step(index, carry):
        group, head = index // 2, index % 2
        start = group * TOGETHER

        def store(unit, values):
            results[start + unit, pl.ds(pl.multiple_of(head * TILE, TILE), TILE)] = values

        some = [start + unit for unit in range(TOGETHER)]
        attend_own(me, some, head, lists_ref, counts_ref, held, store)
        return carry

    def shared_step(group, carry):
        start = group * TOGETHER

        def store(unit, values):
            results[start + unit, 2 * TILE : BACK_ROWS] = values

        some = [start + unit for unit in range(TOGETHER)]
        attend_shared(me, some, lists_ref, counts_ref, held, shared, store)
        return carry

    lax.fori_loop(0, 2 * groups, own_step, 0)
    lax.fori_loop(0, groups, shared_step, 0)
    for mask, out in zip(masks, out_refs):
        out[...] = results[mask]


def attend_rest(me, tables, held, shared, masks):
    back = jax.ShapeDtypeStruct((BACK_ROWS, HEAD_DIM), jnp.bfloat16)
    return pl.pallas_call(
        functools.partial(attend_rest_kernel, masks),
        out_shape=[back] * len(masks),
        in_specs=[SMEM] * 3 + [VMEM] * 2,
        out_specs=[VMEM] * len(masks),
        scratch_shapes=[pltpu.VMEM((len(masks), BACK_ROWS, HEAD_DIM), jnp.bfloat16)],
        compiler_params=PARAMS,
        cost_estimate=attend_cost(3 * len(masks)),
        name="attend_rest",
    )(me, *tables, held, shared)


def attend_cost(units):
    return pl.CostEstimate(
        flops=units * 4 * 4 * TILE * TILE * HEAD_DIM,
        bytes_accessed=units * 4 * TILE * HEAD_DIM * 2,
        transcendentals=units * 4 * TILE * TILE,
    )


def assemble_kernel(masks, heads_pair, me_ref, *rest):
    in_refs = rest[: len(masks)]
    out_ref, sems = rest[len(masks) :]
    me = me_ref[0]
    copies = []

    def add(src, dst):
        copies.append(pltpu.make_async_copy(src, dst, sems.at[len(copies)]))

    for mask, ref in zip(masks, in_refs):
        source = lax.bitwise_xor(me, mask)
        for which in range(2):
            lanes = lanes_of(head_of(source, which, heads_pair))
            add(ref.at[pl.ds(which * TILE, TILE)], out_ref.at[:, lanes])
        lanes = lanes_of(head_of(source, 2, heads_pair))
        half = pl.ds(pl.multiple_of(source % 2 * HALF, HALF), HALF)
        add(ref.at[pl.ds(2 * TILE, HALF)], out_ref.at[half, lanes])
    for copy in copies:
        copy.start()
    for copy in copies:
        copy.wait()


def assemble(me, back, width, masks, heads_pair):
    return pl.pallas_call(
        functools.partial(assemble_kernel, masks, heads_pair),
        out_shape=jax.ShapeDtypeStruct((TILE, width), jnp.bfloat16),
        in_specs=[SMEM] + [VMEM] * len(masks),
        out_specs=pl.BlockSpec(memory_space=pl.ANY),
        scratch_shapes=[pltpu.SemaphoreType.DMA((3 * len(masks),))],
        compiler_params=PARAMS,
        name="assemble",
    )(me, *back)


def exchange(parts, masks, devices):
    return [
        part
        if mask == 0
        else lax.ppermute(part, "ulysses", [(index, index ^ mask) for index in range(devices)])
        for mask, part in zip(masks, parts)
    ]


def local_pairs(query, key, value, query_gain, key_gain, key_blocks, block_counts):
    devices = lax.axis_size("ulysses")
    heads_pair = 2 * HEADS // devices
    index = lax.axis_index("ulysses")
    me = index.astype(jnp.int32).reshape(1)
    far, near = partners(devices)
    masks = [0] + alternate(far, near)
    first, later = far[:TOGETHER], far[TOGETHER:]
    rest = alternate(later, near) + [0]

    leaving = pack(me, query, key, value, query_gain, key_gain, masks, heads_pair)
    early = exchange(leaving[:2], masks[:2], devices)
    early[1], key_blocks, block_counts = lax.optimization_barrier(
        (early[1], key_blocks, block_counts)
    )
    heads = [head_of(index, which, heads_pair) for which in range(3)]
    lists = [lax.dynamic_index_in_dim(key_blocks, head, 0, False) for head in heads]
    counts = [lax.dynamic_index_in_dim(block_counts, head, 0, False) for head in heads]
    tables = (jnp.stack(lists).reshape(-1), jnp.stack(counts).reshape(-1))
    middle = len(masks) - 2
    late, tables = lax.optimization_barrier((leaving[middle:], tables))
    arrived = early + exchange(leaving[2:middle] + late, masks[2:], devices)
    own = collect(me, arrived, masks)
    (other,) = exchange([own], [1], devices)
    held, begun = attend_first(me, tables, arrived, masks, first)
    shared, results = attend_second(me, tables, held, own, other, begun, first)
    back = exchange(results, first, devices)
    back[0], held = lax.optimization_barrier((back[0], held))
    results = attend_rest(me, tables, held, shared, rest)
    back += exchange(results, rest, devices)
    return assemble(me, back, query.shape[1], first + rest, heads_pair)


def pick_group():
    for group_size in (8, 4, 2, 1):
        return group_size
    return 1


def local_any(query, key, value, query_gain, key_gain, key_blocks, block_counts):
    devices = lax.axis_size("ulysses")
    my_index = lax.axis_index("ulysses")
    tok_dev = query.shape[0]
    blocks = tok_dev * devices // TILE
    per_device = HEADS * tok_dev // TILE
    unit_total = HEADS * blocks
    softmax_scale = HEAD_DIM ** (-0.5)
    q_norm = rms_norm(query, query_gain)
    k_norm = rms_norm(key, key_gain)
    marks_all = jnp.arange(devices + 1, dtype=jnp.int32)
    bounds = marks_all * per_device
    span_heads = min(HEADS, (per_device + blocks - 2) // blocks + 1)
    first_head = bounds[:-1] // blocks
    owner_heads = jnp.minimum(
        first_head[:, None] + jnp.arange(span_heads, dtype=jnp.int32)[None, :], HEADS - 1
    )
    packed = (
        jnp.stack([q_norm, k_norm, value], axis=0)
        .reshape(3, tok_dev, HEADS, HEAD_DIM)
        .transpose(2, 0, 1, 3)
    )
    outgoing = (
        packed[owner_heads.T]
        .transpose(0, 2, 1, 3, 4)
        .reshape(span_heads * 3, devices * tok_dev, HEAD_DIM)
    )
    arrived = lax.all_to_all(outgoing, "ulysses", split_axis=1, concat_axis=1, tiled=True)
    resident = arrived.reshape(span_heads, 3, blocks, TILE, HEAD_DIM)
    unit_start = bounds[my_index]
    unit_count = bounds[my_index + 1] - unit_start
    base_head = unit_start // blocks
    group_size = pick_group()
    results = jnp.zeros((span_heads, blocks, TILE, HEAD_DIM), jnp.bfloat16)

    def attend_group(step_index, results):
        local_units = step_index * group_size + jnp.arange(group_size, dtype=jnp.int32)
        unit_live = local_units < unit_count
        unit_ids = jnp.minimum(unit_start + local_units, unit_total - 1)
        unit_heads = unit_ids // blocks
        qblock = unit_ids % blocks
        unit_slots = jnp.clip(unit_heads - base_head, 0, span_heads - 1)
        key_lists = key_blocks[unit_heads, qblock]
        live_count = block_counts[unit_heads, qblock]
        query_matrix = resident[unit_slots, 0, qblock]
        key_panels = resident[unit_slots[:, None], 1, key_lists]
        value_panels = resident[unit_slots[:, None], 2, key_lists]
        logit_matrix = (
            jnp.einsum(
                "gqd,gjkd->gqjk", query_matrix, key_panels, preferred_element_type=jnp.float32
            )
            * softmax_scale
        )
        live_mask = (jnp.arange(KMAX, dtype=jnp.int32)[None, :] < live_count[:, None])[
            :, None, :, None
        ]
        logit_matrix = jnp.where(live_mask, logit_matrix, MASKED)
        row_peak = jnp.max(logit_matrix, axis=(2, 3), keepdims=True)
        weights = jnp.where(live_mask, jnp.exp(logit_matrix - row_peak), 0.0)
        row_denominator = jnp.sum(weights, axis=(2, 3))
        summed = jnp.einsum(
            "gqjk,gjkd->gqd",
            weights.astype(jnp.bfloat16),
            value_panels,
            preferred_element_type=jnp.float32,
        )
        combined = (summed / row_denominator[:, :, None]).astype(jnp.bfloat16)
        write_slots = jnp.where(unit_live, unit_slots, span_heads)
        return results.at[write_slots, qblock].set(combined, mode="drop")

    step_total = (unit_count + group_size - 1) // group_size
    results = lax.fori_loop(0, step_total, attend_group, results)
    leaving = results.reshape(span_heads, blocks * TILE, HEAD_DIM)
    returned = lax.all_to_all(leaving, "ulysses", split_axis=1, concat_axis=0, tiled=True)
    head_range = jnp.arange(HEADS, dtype=jnp.int32)
    selector = (owner_heads.reshape(-1)[None, :] == head_range[:, None]).astype(jnp.bfloat16)
    gathered = jnp.einsum("hs,std->thd", selector, returned, preferred_element_type=jnp.float32)
    return gathered.astype(jnp.bfloat16).reshape(tok_dev, HEADS * HEAD_DIM)


def local(query, *rest):
    devices = lax.axis_size("ulysses")
    power_of_two = devices & (devices - 1) == 0
    five_a_pair = devices % 2 == 0 and devices * 5 == HEADS * 2
    if power_of_two and five_a_pair and query.shape[0] == TILE:
        return local_pairs(query, *rest)
    return local_any(query, *rest)


def solution(mesh):
    in_specs = (
        P(("parts", "ulysses"), None),
        P(("parts", "ulysses"), None),
        P(("parts", "ulysses"), None),
        P(),
        P(),
        P("parts", None, None),
        P("parts", None),
    )
    out_specs = P(("parts", "ulysses"), None)
    return jax.shard_map(local, mesh=mesh, in_specs=in_specs, out_specs=out_specs, check_vma=False)
```

```python
import functools
import math

import jax
import jax.numpy as jnp
from jax import lax
from jax.experimental import pallas as pl
from jax.experimental.pallas import tpu as pltpu
from jax.sharding import PartitionSpec as P

HEADS = 40
HEAD_DIM = 128
TILE = 128
KMAX = 12
HALF = TILE // 2

NORM_EPS = 1e-06
MASKED = -1e30
EXP2_SCALE = HEAD_DIM ** (-0.5) * math.log2(math.e)
SIZES = (2, 4, 6, 8, 10, 12)
TOGETHER = 8
VMEM_LIMIT = 12 * 1024 * 1024
PACK_VMEM_LIMIT = 58 * 1024 * 1024

HEAD_ROWS = 3 * TILE
SHARED_Q = 2 * HEAD_ROWS
SHARED_KV = SHARED_Q + HALF
ROWS = SHARED_KV + TILE
BACK_ROWS = 2 * TILE + HALF

HBM = pl.BlockSpec(memory_space=pltpu.HBM)
SMEM = pl.BlockSpec(memory_space=pltpu.SMEM)
VMEM = pl.BlockSpec(memory_space=pltpu.VMEM)
PARAMS = pltpu.CompilerParams(vmem_limit_bytes=VMEM_LIMIT)


def rms_norm(values_in, gain):
    widened = values_in.astype(jnp.float32)
    inverse = lax.rsqrt(jnp.mean(widened * widened, axis=-1, keepdims=True) + NORM_EPS)
    return (widened * inverse * gain).astype(jnp.bfloat16)


def head_of(device, which, heads_pair):
    base = (device // 2) * heads_pair
    core = device % 2
    if which == 2:
        return base + 2
    return base + core * 3 + which


def lanes_of(head):
    return pl.ds(pl.multiple_of(head * HEAD_DIM, HEAD_DIM), HEAD_DIM)


def alternate(far, near):
    order = []
    for index in range(max(len(far), len(near))):
        order += far[index : index + 1] + near[index : index + 1]
    return order


def even_first(masks):
    return sorted(masks, key=lambda mask: (mask % 2, mask))


def partners(devices):
    half, quarter = devices // 2, devices // 4
    far = even_first(range(half, devices))
    near = alternate(even_first(range(quarter, half)), even_first(range(1, quarter)))
    return far, near


def pack_kernel(masks, heads_pair, me_ref, q_hbm, k_hbm, v_hbm, qg_hbm, kg_hbm, *rest):
    out_refs = rest[: len(masks)]
    q_ref, k_ref, v_ref, qg_ref, kg_ref, q_norm, k_norm, sems = rest[len(masks) :]
    me = me_ref[0]
    loads = [
        pltpu.make_async_copy(src, dst, sems.at[at])
        for at, (src, dst) in enumerate(
            (
                (qg_hbm, qg_ref),
                (kg_hbm, kg_ref),
                (q_hbm, q_ref),
                (k_hbm, k_ref),
                (v_hbm, v_ref),
            )
        )
    ]
    for load in loads:
        load.start()
    loads[0].wait()
    loads[1].wait()
    width = q_ref.shape[1]
    step = 8 * HEAD_DIM
    for load, src, gain, dst in (
        (loads[2], q_ref, qg_ref, q_norm),
        (loads[3], k_ref, kg_ref, k_norm),
    ):
        load.wait()
        total = jnp.zeros((TILE, HEAD_DIM), jnp.float32)
        for lane in range(0, width, HEAD_DIM):
            part = src[:, lane : lane + HEAD_DIM].astype(jnp.float32)
            total += part * part
        mean = jnp.sum(total, axis=1, keepdims=True) * (1.0 / width)
        inverse = lax.rsqrt(mean + NORM_EPS)
        for lane in range(0, width, step):
            part = src[:, lane : lane + step].astype(jnp.float32)
            dst[:, lane : lane + step] = (part * inverse * gain[:, lane : lane + step]).astype(
                jnp.bfloat16
            )
    loads[4].wait()
    for mask, out in zip(masks, out_refs):
        to = lax.bitwise_xor(me, mask)
        core = to % 2
        for which in range(2):
            lanes = lanes_of(head_of(to, which, heads_pair))
            row = which * HEAD_ROWS
            out[row : row + TILE] = q_norm[:, lanes]
            out[row + TILE : row + 2 * TILE] = k_norm[:, lanes]
            out[row + 2 * TILE : row + 3 * TILE] = v_ref[:, lanes]
        lanes = lanes_of(head_of(to, 2, heads_pair))
        half = pl.ds(pl.multiple_of(core * HALF, HALF), HALF)
        out[SHARED_Q:SHARED_KV] = q_norm[half, lanes]

        @pl.when(core == 0)
        def _(out=out, lanes=lanes):
            out[SHARED_KV:ROWS] = k_norm[:, lanes]

        @pl.when(core == 1)
        def _(out=out, lanes=lanes):
            out[SHARED_KV:ROWS] = v_ref[:, lanes]


def pack(me, query, key, value, query_gain, key_gain, masks, heads_pair):
    gain = pltpu.VMEM((1, query.shape[1]), jnp.float32)
    return pl.pallas_call(
        functools.partial(pack_kernel, masks, heads_pair),
        out_shape=[jax.ShapeDtypeStruct((ROWS, HEAD_DIM), jnp.bfloat16)] * len(masks),
        in_specs=[SMEM] + [HBM] * 5,
        out_specs=[VMEM] * len(masks),
        scratch_shapes=[pltpu.VMEM(query.shape, jnp.bfloat16)] * 3
        + [gain] * 2
        + [pltpu.VMEM(query.shape, jnp.bfloat16)] * 2
        + [pltpu.SemaphoreType.DMA((5,))],
        compiler_params=pltpu.CompilerParams(vmem_limit_bytes=PACK_VMEM_LIMIT),
        name="norm_pack",
    )(me, query, key, value, query_gain[None, :], key_gain[None, :])


def collect_kernel(masks, me_ref, *rest):
    in_refs, out_ref = rest[: len(masks)], rest[len(masks)]
    me = me_ref[0]
    for mask, ref in zip(masks, in_refs):
        out_ref[lax.bitwise_xor(me, mask)] = ref[SHARED_KV:ROWS]


def collect(me, arrived, masks):
    return pl.pallas_call(
        functools.partial(collect_kernel, masks),
        out_shape=jax.ShapeDtypeStruct((len(masks), TILE, HEAD_DIM), jnp.bfloat16),
        in_specs=[SMEM] + [VMEM] * len(masks),
        out_specs=VMEM,
        compiler_params=PARAMS,
        name="collect_shared",
    )(me, *arrived)


def attend_together(counts, list_at, query_of, key_of, value_of, store):
    longest = functools.reduce(jnp.maximum, counts)
    least = 0
    for size in SIZES:

        @pl.when((longest > least) & (longest <= size))
        def _(size=size):
            column = lax.broadcasted_iota(jnp.int32, (1, size * TILE), 1)
            units = range(len(counts))
            picked = [[list_at(unit, slot) for slot in range(size)] for unit in units]
            scores = []
            for unit in units:
                keys = jnp.concatenate([key_of(block) for block in picked[unit]], axis=0)
                scores.append(
                    lax.dot_general(
                        query_of(unit),
                        keys,
                        (((1,), (1,)), ((), ())),
                        preferred_element_type=jnp.float32,
                    )
                    + jnp.where(column < counts[unit] * TILE, 0.0, MASKED)
                )
            weights, totals = [], []
            for unit in units:
                peak = jnp.max(scores[unit], axis=1, keepdims=True)
                wide = jnp.exp2((scores[unit] - peak) * EXP2_SCALE)
                totals.append(jnp.sum(wide, axis=1, keepdims=True))
                weights.append(wide.astype(jnp.bfloat16))
            summed = []
            for unit in units:
                values = jnp.concatenate([value_of(block) for block in picked[unit]], axis=0)
                summed.append(
                    jnp.dot(weights[unit], values, preferred_element_type=jnp.float32)
                )
            for unit in units:
                store(unit, (summed[unit] / totals[unit]).astype(jnp.bfloat16))

        least = size


def attend_own(me, masks, head, lists_ref, counts_ref, held, store):
    blocks = [lax.bitwise_xor(me, mask) for mask in masks]
    devices = held.shape[0]
    row = head * HEAD_ROWS
    rows = [pl.ds(pl.multiple_of(row + part * TILE, TILE), TILE) for part in range(3)]
    attend_together(
        [counts_ref[head * devices + block] for block in blocks],
        lambda unit, slot: lists_ref[(head * devices + blocks[unit]) * KMAX + slot],
        lambda unit: held[blocks[unit], rows[0]],
        lambda at: held[at, rows[1]],
        lambda at: held[at, rows[2]],
        store,
    )


def attend_shared(me, masks, lists_ref, counts_ref, held, shared, store):
    blocks = [lax.bitwise_xor(me, mask) for mask in masks]
    devices = held.shape[0]
    attend_together(
        [counts_ref[2 * devices + block] for block in blocks],
        lambda unit, slot: lists_ref[(2 * devices + blocks[unit]) * KMAX + slot],
        lambda unit: held[blocks[unit], SHARED_Q:SHARED_KV],
        lambda at: shared[0, at],
        lambda at: shared[1, at],
        store,
    )


def attend_first_kernel(masks, first, me_ref, lists_ref, counts_ref, *rest):
    in_refs = rest[: len(masks)]
    held, results = rest[len(masks) :]
    me = me_ref[0]
    for mask, ref in zip(masks, in_refs):
        held[lax.bitwise_xor(me, mask)] = ref[0:SHARED_KV]

    def step(index, carry):
        start, head = index // 2 * TOGETHER, index % 2

        def store(unit, values):
            results[start + unit, pl.ds(pl.multiple_of(head * TILE, TILE), TILE)] = values

        some = [min(first) + start + unit for unit in range(TOGETHER)]
        attend_own(me, some, head, lists_ref, counts_ref, held, store)
        return carry

    lax.fori_loop(0, 2 * len(first) // TOGETHER, step, 0)


def attend_first(me, tables, arrived, masks, first):
    devices = len(masks)
    return pl.pallas_call(
        functools.partial(attend_first_kernel, masks, first),
        out_shape=[
            jax.ShapeDtypeStruct((devices, SHARED_KV, HEAD_DIM), jnp.bfloat16),
            jax.ShapeDtypeStruct((len(first), 2 * TILE, HEAD_DIM), jnp.bfloat16),
        ],
        in_specs=[SMEM] * 3 + [VMEM] * devices,
        out_specs=[VMEM] * 2,
        compiler_params=PARAMS,
        cost_estimate=attend_cost(2 * len(first)),
        name="attend_first",
    )(me, *tables, *arrived)


def attend_second_kernel(
    first, me_ref, lists_ref, counts_ref, held, own_ref, other_ref, begun, shared, *rest
):
    out_refs, results = rest[: len(first)], rest[len(first)]
    me = me_ref[0]
    core = me % 2
    shared[core] = own_ref[...]
    shared[1 - core] = other_ref[...]

    def step(group, carry):
        start = group * TOGETHER

        def store(unit, values):
            results[start + unit] = values

        some = [min(first) + start + unit for unit in range(TOGETHER)]
        attend_shared(me, some, lists_ref, counts_ref, held, shared, store)
        return carry

    lax.fori_loop(0, len(first) // TOGETHER, step, 0)
    for mask, out in zip(first, out_refs):
        out[0 : 2 * TILE] = begun[mask - min(first)]
        out[2 * TILE : BACK_ROWS] = results[mask - min(first)]


def attend_second(me, tables, held, own, other, begun, first):
    devices = held.shape[0]
    back = jax.ShapeDtypeStruct((BACK_ROWS, HEAD_DIM), jnp.bfloat16)
    outs = pl.pallas_call(
        functools.partial(attend_second_kernel, first),
        out_shape=[jax.ShapeDtypeStruct((2, devices, TILE, HEAD_DIM), jnp.bfloat16)]
        + [back] * len(first),
        in_specs=[SMEM] * 3 + [VMEM] * 4,
        out_specs=[VMEM] * (1 + len(first)),
        scratch_shapes=[pltpu.VMEM((len(first), HALF, HEAD_DIM), jnp.bfloat16)],
        compiler_params=PARAMS,
        cost_estimate=attend_cost(len(first)),
        name="attend_second",
    )(me, *tables, held, own, other, begun)
    return outs[0], list(outs[1:])


def attend_cost(units):
    return pl.CostEstimate(
        flops=units * 4 * 4 * TILE * TILE * HEAD_DIM,
        bytes_accessed=units * 4 * TILE * HEAD_DIM * 2,
        transcendentals=units * 4 * TILE * TILE,
    )


def assemble_kernel(masks, heads_pair, me_ref, *rest):
    in_refs = rest[: len(masks)]
    out_ref, sems = rest[len(masks) :]
    me = me_ref[0]
    copies = []

    def add(src, dst):
        copies.append(pltpu.make_async_copy(src, dst, sems.at[len(copies)]))

    for mask, ref in zip(masks, in_refs):
        source = lax.bitwise_xor(me, mask)
        for which in range(2):
            lanes = lanes_of(head_of(source, which, heads_pair))
            add(ref.at[pl.ds(which * TILE, TILE)], out_ref.at[:, lanes])
        lanes = lanes_of(head_of(source, 2, heads_pair))
        half = pl.ds(pl.multiple_of(source % 2 * HALF, HALF), HALF)
        add(ref.at[pl.ds(2 * TILE, HALF)], out_ref.at[half, lanes])
    for copy in copies:
        copy.start()
    for copy in copies:
        copy.wait()


def assemble(me, back, width, masks, heads_pair):
    return pl.pallas_call(
        functools.partial(assemble_kernel, masks, heads_pair),
        out_shape=jax.ShapeDtypeStruct((TILE, width), jnp.bfloat16),
        in_specs=[SMEM] + [VMEM] * len(masks),
        out_specs=pl.BlockSpec(memory_space=pl.ANY),
        scratch_shapes=[pltpu.SemaphoreType.DMA((3 * len(masks),))],
        compiler_params=PARAMS,
        name="assemble",
    )(me, *back)


def exchange(parts, masks, devices):
    return [
        part
        if mask == 0
        else lax.ppermute(part, "ulysses", [(index, index ^ mask) for index in range(devices)])
        for mask, part in zip(masks, parts)
    ]


def local_pairs(query, key, value, query_gain, key_gain, key_blocks, block_counts):
    devices = lax.axis_size("ulysses")
    heads_pair = 2 * HEADS // devices
    index = lax.axis_index("ulysses")
    me = index.astype(jnp.int32).reshape(1)
    far, near = partners(devices)
    masks = [0] + alternate(far, near)

    leaving = pack(me, query, key, value, query_gain, key_gain, masks, heads_pair)
    early = exchange(leaving[:2], masks[:2], devices)
    early[1], key_blocks, block_counts = lax.optimization_barrier(
        (early[1], key_blocks, block_counts)
    )
    heads = [head_of(index, which, heads_pair) for which in range(3)]
    lists = [lax.dynamic_index_in_dim(key_blocks, head, 0, False) for head in heads]
    counts = [lax.dynamic_index_in_dim(block_counts, head, 0, False) for head in heads]
    tables = (jnp.stack(lists).reshape(-1), jnp.stack(counts).reshape(-1))
    middle = len(masks) - 2
    late, tables = lax.optimization_barrier((leaving[middle:], tables))
    arrived = early + exchange(leaving[2:middle] + late, masks[2:], devices)
    own = collect(me, arrived, masks)
    (other,) = exchange([own], [1], devices)
    held, begun = attend_first(me, tables, arrived, masks, masks)
    _, results = attend_second(me, tables, held, own, other, begun, masks)
    back = exchange(results, masks, devices)
    return assemble(me, back, query.shape[1], masks, heads_pair)


def pick_group():
    for group_size in (8, 4, 2, 1):
        return group_size
    return 1


def local_any(query, key, value, query_gain, key_gain, key_blocks, block_counts):
    devices = lax.axis_size("ulysses")
    my_index = lax.axis_index("ulysses")
    tok_dev = query.shape[0]
    blocks = tok_dev * devices // TILE
    per_device = HEADS * tok_dev // TILE
    unit_total = HEADS * blocks
    softmax_scale = HEAD_DIM ** (-0.5)
    q_norm = rms_norm(query, query_gain)
    k_norm = rms_norm(key, key_gain)
    marks_all = jnp.arange(devices + 1, dtype=jnp.int32)
    bounds = marks_all * per_device
    span_heads = min(HEADS, (per_device + blocks - 2) // blocks + 1)
    first_head = bounds[:-1] // blocks
    owner_heads = jnp.minimum(
        first_head[:, None] + jnp.arange(span_heads, dtype=jnp.int32)[None, :], HEADS - 1
    )
    packed = (
        jnp.stack([q_norm, k_norm, value], axis=0)
        .reshape(3, tok_dev, HEADS, HEAD_DIM)
        .transpose(2, 0, 1, 3)
    )
    outgoing = (
        packed[owner_heads.T]
        .transpose(0, 2, 1, 3, 4)
        .reshape(span_heads * 3, devices * tok_dev, HEAD_DIM)
    )
    arrived = lax.all_to_all(outgoing, "ulysses", split_axis=1, concat_axis=1, tiled=True)
    resident = arrived.reshape(span_heads, 3, blocks, TILE, HEAD_DIM)
    unit_start = bounds[my_index]
    unit_count = bounds[my_index + 1] - unit_start
    base_head = unit_start // blocks
    group_size = pick_group()
    results = jnp.zeros((span_heads, blocks, TILE, HEAD_DIM), jnp.bfloat16)

    def attend_group(step_index, results):
        local_units = step_index * group_size + jnp.arange(group_size, dtype=jnp.int32)
        unit_live = local_units < unit_count
        unit_ids = jnp.minimum(unit_start + local_units, unit_total - 1)
        unit_heads = unit_ids // blocks
        qblock = unit_ids % blocks
        unit_slots = jnp.clip(unit_heads - base_head, 0, span_heads - 1)
        key_lists = key_blocks[unit_heads, qblock]
        live_count = block_counts[unit_heads, qblock]
        query_matrix = resident[unit_slots, 0, qblock]
        key_panels = resident[unit_slots[:, None], 1, key_lists]
        value_panels = resident[unit_slots[:, None], 2, key_lists]
        logit_matrix = (
            jnp.einsum(
                "gqd,gjkd->gqjk", query_matrix, key_panels, preferred_element_type=jnp.float32
            )
            * softmax_scale
        )
        live_mask = (jnp.arange(KMAX, dtype=jnp.int32)[None, :] < live_count[:, None])[
            :, None, :, None
        ]
        logit_matrix = jnp.where(live_mask, logit_matrix, MASKED)
        row_peak = jnp.max(logit_matrix, axis=(2, 3), keepdims=True)
        weights = jnp.where(live_mask, jnp.exp(logit_matrix - row_peak), 0.0)
        row_denominator = jnp.sum(weights, axis=(2, 3))
        summed = jnp.einsum(
            "gqjk,gjkd->gqd",
            weights.astype(jnp.bfloat16),
            value_panels,
            preferred_element_type=jnp.float32,
        )
        combined = (summed / row_denominator[:, :, None]).astype(jnp.bfloat16)
        write_slots = jnp.where(unit_live, unit_slots, span_heads)
        return results.at[write_slots, qblock].set(combined, mode="drop")

    step_total = (unit_count + group_size - 1) // group_size
    results = lax.fori_loop(0, step_total, attend_group, results)
    leaving = results.reshape(span_heads, blocks * TILE, HEAD_DIM)
    returned = lax.all_to_all(leaving, "ulysses", split_axis=1, concat_axis=0, tiled=True)
    head_range = jnp.arange(HEADS, dtype=jnp.int32)
    selector = (owner_heads.reshape(-1)[None, :] == head_range[:, None]).astype(jnp.bfloat16)
    gathered = jnp.einsum("hs,std->thd", selector, returned, preferred_element_type=jnp.float32)
    return gathered.astype(jnp.bfloat16).reshape(tok_dev, HEADS * HEAD_DIM)


def local(query, *rest):
    devices = lax.axis_size("ulysses")
    power_of_two = devices & (devices - 1) == 0
    five_a_pair = devices % 2 == 0 and devices * 5 == HEADS * 2
    if power_of_two and five_a_pair and query.shape[0] == TILE:
        return local_pairs(query, *rest)
    return local_any(query, *rest)


def solution(mesh):
    in_specs = (
        P(("parts", "ulysses"), None),
        P(("parts", "ulysses"), None),
        P(("parts", "ulysses"), None),
        P(),
        P(),
        P("parts", None, None),
        P("parts", None),
    )
    out_specs = P(("parts", "ulysses"), None)
    return jax.shard_map(local, mesh=mesh, in_specs=in_specs, out_specs=out_specs, check_vma=False)
```
